32 devices in a mesh: region: 4 (over y, core), sub: 8 (over z, x).
Axes of the slice: x: 2, y: 2, z: 4, core: 2. Of those that a mesh axis runs over, the one named last changes fastest.
Arguments:
- probes: bfloat16 [32, 425984], P(None, ('region', 'sub')), may hold values from -6 to 6
- blocks: bfloat16 [3328, 3, 128, 128], P(('region', 'sub')), may hold values from -0.109375 to 0.109375
- col_slot: int32 [3328, 3], P(('region', 'sub')), may hold values from 0 to 127, as said below
- send_sub: int32 [32, 2, 8], P(('region', 'sub')), may hold values from -1 to 103, as said below
- send_reg: int32 [32, 2, 4], P(('region', 'sub')), may hold values from -1 to 103, as said below
- coeffs: float32 [9], replicated, may hold values from 0.3 to 1
Outputs:
- filtered: float32 [32, 425984], P(None, ('region', 'sub'))
The draws below stay inside these ranges and needn't reach their ends.
Inputs may be any that keep to these rules, and one draw needn't show every extreme that they name: `col_slot`: entry 0 of each block row names the row's own block. Slots from 104 on name received blocks in this order: 8 from the lower sub neighbour, 8 from the upper sub neighbour, 4 from the lower region neighbour, 4 from the upper one; only received slots that the sender fills are named, and each of those is named by some row. send_sub[d, 0] lists rows sent to sub index one lower in the same region, send_sub[d, 1] to one higher: distinct rows first, then -1; devices at the ends of the sub axis send nothing outward; some list is full. send_reg[d, 0] lists rows sent to the same sub index in the region one lower, send_reg[d, 1] one higher: distinct rows first, then -1; the first and last regions send nothing outward; some list is full.
All inputs are finite; a program needn't handle non-finite values.
Results may differ from the reference program's by a relative error of at most 0.0065.
Values may be sent and summed in bfloat16 or wider, within the bound.
No kernel may reach another device: no remote copies, remote signals or barrier semaphores. Data moves between devices by JAX's collectives and lax.ppermute only.
A program may use at most 128 MiB of HBM per device.

```python
import jax
import jax.numpy as jnp
import numpy as np
from jax import lax

BLK = 128
NNZ = 3
PROBES = 32
DEG = 8
ROWS_DEV = 104
HS = 8
HR = 4
BLOCK_ROWS = 3328
NODES = 425984
N_REGION = 4
N_SUB = 8


def halo_plan(key):
    device_total = N_REGION * N_SUB
    device_ids = jnp.arange(device_total)
    sub_index = device_ids % N_SUB
    region_index = device_ids // N_SUB
    sub_counts = jax.random.randint(jax.random.fold_in(key, 1), (device_total, 2), 1, HS + 1)
    sub_counts = sub_counts.at[0, 1].set(HS).at[1, 0].set(HS)
    sub_counts = jnp.stack([jnp.where(sub_index == 0, 0, sub_counts[:, 0]), jnp.where(sub_index == N_SUB - 1, 0, sub_counts[:, 1])], 1)
    reg_counts = jax.random.randint(jax.random.fold_in(key, 2), (device_total, 2), 1, HR + 1)
    reg_counts = reg_counts.at[0, 1].set(HR).at[N_SUB, 0].set(HR)
    reg_counts = jnp.stack([jnp.where(region_index == 0, 0, reg_counts[:, 0]), jnp.where(region_index == N_REGION - 1, 0, reg_counts[:, 1])], 1)

    def row_lists(base_key, width, counts):
        keys = jax.random.split(base_key, device_total * 2)
        orders = jax.vmap(lambda one_key: jax.random.permutation(one_key, ROWS_DEV))(keys).reshape(device_total, 2, ROWS_DEV)
        rotate = ROWS_DEV - 1 - orders[0, :, 0]
        orders = orders.at[0].set((orders[0] + rotate[:, None]) % ROWS_DEV)
        position = jnp.arange(width)[None, None, :]
        return jnp.where(position < counts[:, :, None], orders[:, :, :width], -1).astype(jnp.int32)
    send_sub = row_lists(jax.random.fold_in(key, 3), HS, sub_counts)
    send_reg = row_lists(jax.random.fold_in(key, 4), HR, reg_counts)
    grid_sub = sub_counts.reshape(N_REGION, N_SUB, 2)
    grid_reg = reg_counts.reshape(N_REGION, N_SUB, 2)
    zero_column = jnp.zeros((N_REGION, 1), grid_sub.dtype)
    zero_row = jnp.zeros((1, N_SUB), grid_reg.dtype)
    recv_first = jnp.concatenate([zero_column, grid_sub[:, :-1, 1]], 1).reshape(device_total)
    recv_second = jnp.concatenate([grid_sub[:, 1:, 0], zero_column], 1).reshape(device_total)
    recv_third = jnp.concatenate([zero_row, grid_reg[:-1, :, 1]], 0).reshape(device_total)
    recv_fourth = jnp.concatenate([grid_reg[1:, :, 0], zero_row], 0).reshape(device_total)
    recv_counts = jnp.stack([recv_first, recv_second, recv_third, recv_fourth], 1)
    segment = np.array([0] * HS + [1] * HS + [2] * HR + [3] * HR, dtype=np.int32)
    inside = np.array(list(range(HS)) + list(range(HS)) + list(range(HR)) + list(range(HR)), dtype=np.int32)
    received = 2 * HS + 2 * HR
    live = jnp.asarray(inside)[None, :] < recv_counts[:, segment]
    extra_count = ROWS_DEV * (NNZ - 1)
    filler = jax.random.randint(jax.random.fold_in(key, 5), (device_total, extra_count), 0, ROWS_DEV)
    place_keys = jax.random.split(jax.random.fold_in(key, 6), device_total)
    places = jax.vmap(lambda one_key: jax.random.permutation(one_key, extra_count))(place_keys)[:, :received]
    chosen = jnp.where(live, ROWS_DEV + jnp.arange(received)[None, :], jnp.take_along_axis(filler, places, axis=1))
    extra = filler.at[device_ids[:, None], places].set(chosen)
    extra = extra.reshape(device_total, ROWS_DEV, NNZ - 1)
    own = jnp.broadcast_to(jnp.arange(ROWS_DEV)[None, :, None], (device_total, ROWS_DEV, 1))
    col_slot = jnp.concatenate([own, extra], 2).reshape(device_total * ROWS_DEV, NNZ).astype(jnp.int32)
    return (send_sub, send_reg, col_slot)


def draw_col_slot(key, part):
    return halo_plan(key)[2]


def draw_send_sub(key, part):
    return halo_plan(key)[0]


def draw_send_reg(key, part):
    return halo_plan(key)[1]


def block_levels(rng, shape, cuts, smallest, top_value):
    loudness, own = 1.0, jax.random.fold_in(rng, 6)
    for axis_at, parts in cuts:
        draws = jnp.exp(jax.random.uniform(jax.random.fold_in(own, axis_at), (parts,), jnp.float32, smallest / len(cuts), top_value / len(cuts)))
        loudness = loudness * jnp.repeat(draws, shape[axis_at] // parts).reshape([-1 if axis == axis_at else 1 for axis in range(len(shape))])
    return loudness


def noise(rng, extent, deviation, most, cuts=(), kind=jnp.bfloat16):
    drawn = deviation * jax.random.normal(rng, extent, jnp.float32)
    if cuts:
        drawn = drawn * block_levels(rng, extent, cuts, -0.22, 0.18)
    return jnp.clip(drawn, -most, most).astype(kind)


def setup_inputs(seed: int = 0) -> dict:
    key_of = jax.random.split(jax.random.key(seed), 7)
    probes = noise(key_of[0], (PROBES, NODES), 1.0, 6.0, ((1, 32),))
    blocks = noise(key_of[1], (BLOCK_ROWS, NNZ, BLK, BLK), (8 * NNZ * BLK) ** -0.5, 0.109375, ((0, 32),))
    col_slot = draw_col_slot(jax.random.fold_in(key_of[6], 71), 0)
    send_sub = draw_send_sub(jax.random.fold_in(key_of[6], 71), 0)
    send_reg = draw_send_reg(jax.random.fold_in(key_of[6], 71), 0)
    coeffs = jnp.clip(jax.random.uniform(key_of[5], (DEG + 1,), jnp.float32, 0.3, 1.0), 0.3, 1.0)
    return {"probes": probes, "blocks": blocks, "col_slot": col_slot, "send_sub": send_sub, "send_reg": send_reg, "coeffs": coeffs}


def column_ids(col_slot, send_sub, send_reg):
    device_total = N_REGION * N_SUB
    slots = col_slot.reshape(device_total, ROWS_DEV, NNZ)
    device_ids = jnp.arange(device_total, dtype=jnp.int32)[:, None, None]
    own_ids = device_ids * ROWS_DEV + slots
    lower_sub = jnp.clip(device_ids - 1, 0, device_total - 1)
    upper_sub = jnp.clip(device_ids + 1, 0, device_total - 1)
    lower_reg = jnp.clip(device_ids - N_SUB, 0, device_total - 1)
    upper_reg = jnp.clip(device_ids + N_SUB, 0, device_total - 1)
    offset = slots - ROWS_DEV
    first_pos = jnp.clip(offset, 0, HS - 1)
    second_pos = jnp.clip(offset - HS, 0, HS - 1)
    third_pos = jnp.clip(offset - 2 * HS, 0, HR - 1)
    fourth_pos = jnp.clip(offset - 2 * HS - HR, 0, HR - 1)
    first_ids = lower_sub * ROWS_DEV + send_sub[lower_sub, 1, first_pos]
    second_ids = upper_sub * ROWS_DEV + send_sub[upper_sub, 0, second_pos]
    third_ids = lower_reg * ROWS_DEV + send_reg[lower_reg, 1, third_pos]
    fourth_ids = upper_reg * ROWS_DEV + send_reg[upper_reg, 0, fourth_pos]
    result = jnp.where(offset < 2 * HS + HR, third_ids, fourth_ids)
    result = jnp.where(offset < 2 * HS, second_ids, result)
    result = jnp.where(offset < HS, first_ids, result)
    result = jnp.where(offset < 0, own_ids, result)
    return result.astype(jnp.int32)


def apply_operator(packed, blocks_dev, global_ids):
    vectors = packed.reshape(PROBES, BLOCK_ROWS, BLK)

    def one_device(items):
        block_group, id_group = items
        taken = jnp.take(vectors, id_group, axis=1)
        return jnp.einsum("pnkc,nkac->pna", taken.astype(jnp.float32), block_group.astype(jnp.float32))

    result = lax.map(one_device, (blocks_dev, global_ids))
    return jnp.transpose(result, (1, 0, 2, 3)).reshape(PROBES, NODES)


def reference(probes, blocks, col_slot, send_sub, send_reg, coeffs):
    device_total = N_REGION * N_SUB
    global_ids = column_ids(col_slot, send_sub, send_reg)
    blocks_dev = blocks.reshape(device_total, ROWS_DEV, NNZ, BLK, BLK)
    previous = probes.astype(jnp.float32)
    total = coeffs[0] * previous
    current = apply_operator(previous.astype(jnp.bfloat16), blocks_dev, global_ids)
    total = total + coeffs[1] * current
    for degree_step in range(2, DEG + 1):
        following = 2.0 * apply_operator(current.astype(jnp.bfloat16), blocks_dev, global_ids) - previous
        total = total + coeffs[degree_step] * following
        previous, current = current, following
    return total
```

```python
import functools

import jax
import jax.numpy as jnp
from jax import lax
from jax.experimental import pallas as pl
from jax.experimental.pallas import tpu as pltpu
from jax.sharding import PartitionSpec as P

DEG = 8
BATCH = 8
SMEM = pl.BlockSpec(memory_space=pltpu.SMEM)
VMEM = pl.BlockSpec(memory_space=pltpu.VMEM)
HBM = pl.BlockSpec(memory_space=pl.ANY)
F32, BF16, I32 = jnp.float32, jnp.bfloat16, jnp.int32


def dot(x, b):
    return lax.dot_general(x, b, (((1,), (0,)), ((), ())), preferred_element_type=F32)


def in_vmem(x):
    return pltpu.with_memory_space_constraint(x, pltpu.VMEM)


def divisor(n, most):
    return next(d for d in range(min(n, most), 0, -1) if n % d == 0)


def swaps():
    regions, subs = lax.axis_size("region"), lax.axis_size("sub")

    def route(mate):
        pairs = []
        for r in range(regions):
            for s in range(subs):
                m = mate(r, s)
                if m is not None:
                    pairs.append((r * subs + s, m[0] * subs + m[1]))
        return pairs

    def idle_sub(r, s):
        return (r ^ 1, s) if r ^ 1 < regions else None

    def sub_even(r, s):
        return (r, s ^ 1) if s ^ 1 < subs else idle_sub(r, s)

    def sub_odd(r, s):
        m = ((s - 1) ^ 1) + 1
        return (r, m) if s > 0 and m < subs else idle_sub(r, s)

    def reg_even(r, s):
        return (r ^ 1, s) if r ^ 1 < regions else None

    def reg_odd(r, s):
        m = ((r - 1) ^ 1) + 1
        if r > 0 and m < regions:
            return (m, s)
        return (regions - 1 - r, s) if regions % 2 == 0 else None

    return [route(f) for f in (sub_even, sub_odd, reg_even, reg_odd)]


def exchange(sends):
    routes = swaps()
    order = (0, 1, 3, 2)
    got = [None] * 4
    for i in order:
        got[i] = lax.ppermute(sends[i], ("region", "sub"), routes[i])
    return got


class Layout:
    def __init__(self, rows, hs, hr):
        self.rows, self.hs, self.hr = rows, hs, hr
        self.halo = 2 * hs + 2 * hr
        self.starts = (0, hs, 2 * hs, 2 * hs + hr)
        self.counts = (hs, hs, hr, hr)
        self.loc = 0
        self.far = 3 * rows
        self.tab = self.far + 2 * rows + BATCH
        self.out = self.tab + self.halo
        self.n_far = self.out + 2 * self.halo + BATCH
        self.n_out = self.n_far + 1
        self.size = self.n_out + 1


def pack(place, block, got):
    return place + block * 1024 + got * (1 << 20)


def unpack(code):
    return code & 1023, (code >> 10) & 1023, code >> 20


def send_row(lay, sub_ref, reg_ref, j):
    rp, sp = lax.axis_index("region") % 2, lax.axis_index("sub") % 2
    hs, hr = lay.hs, lay.hr
    if j < hs:
        row = sub_ref[0, 1 - sp, j]
    elif j < 2 * hs:
        row = sub_ref[0, sp, j - hs]
    elif j < 2 * hs + hr:
        row = reg_ref[0, 1 - rp, j - 2 * hs]
    else:
        row = reg_ref[0, rp, j - 2 * hs - hr]
    return jnp.maximum(row, 0)


def first_send_kernel(lay, sub_ref, reg_ref, probes_ref, *send_refs):
    for n, (start, count) in enumerate(zip(lay.starts, lay.counts)):
        for j in range(count):
            row = send_row(lay, sub_ref, reg_ref, start + j)
            send_refs[n][j] = probes_ref[:, pl.ds(pl.multiple_of(row * 128, 128), 128)]


def prologue_kernel(lay, chunk, slot_ref, sub_ref, reg_ref, coeff_ref, probes_ref, blocks_ref,
                    bt_ref, x_ref, y_ref, t_ref, ext_ref, info_ref, raw, sems):
    rows = lay.rows
    chunks = rows // chunk
    copies = [
        pltpu.make_async_copy(blocks_ref.at[pl.ds(c * chunk, chunk)], raw.at[pl.ds(c * chunk, chunk)], sems.at[c])
        for c in range(chunks)
    ]
    for copy in copies:
        copy.start()
    rp, sp = lax.axis_index("region") % 2, lax.axis_index("sub") % 2
    hs, hr = lay.hs, lay.hr

    def received(slot):
        o = slot - rows
        sub_at = jnp.where(sp == 1, o, jnp.where(o < hs, o + hs, o - hs))
        q = o - 2 * hs
        reg_at = jnp.where(rp == 1, o, jnp.where(q < hr, o + hr, o - hr))
        return jnp.where(o < 2 * hs, sub_at, reg_at)

    c0 = coeff_ref[0]
    for i in range(rows):
        v = probes_ref[:, i * 128:(i + 1) * 128]
        ext_ref[i] = v
        x_ref[i] = v.astype(F32)
        t_ref[i] = c0 * v.astype(F32)
    ext_ref[rows] = jnp.zeros_like(ext_ref[rows])
    y_ref[rows] = jnp.zeros_like(y_ref[rows])
    x_ref[rows] = jnp.zeros_like(x_ref[rows])

    def many(c, far):
        pltpu.make_async_copy(blocks_ref.at[pl.ds(c * chunk, chunk)], raw.at[pl.ds(c * chunk, chunk)], sems.at[c]).wait()
        for u in range(chunk):
            i = c * chunk + u
            at = []
            for k in range(3):
                slot = slot_ref[i, k]
                at.append(jnp.where(slot < rows, slot, rows))
                info_ref[lay.loc + 3 * i + k] = at[k]
                if k > 0:
                    info_ref[lay.far + far] = pack(i, 3 * i + k, jnp.maximum(received(slot), 0))
                    far = far + jnp.where(slot < rows, 0, 1)
            turned = [raw[i, k].T for k in range(3)]
            for k in range(3):
                bt_ref[3 * i + k] = turned[k]
            x = jnp.concatenate([ext_ref[at[k]] for k in range(3)], 1)
            y_ref[i] = dot(x, jnp.concatenate(turned, 0))
        return far

    far = lax.fori_loop(0, chunks, many, jnp.int32(0))
    for u in range(BATCH):
        info_ref[lay.far + far + u] = pack(rows, 0, 0)
    info_ref[lay.n_far] = far
    out = jnp.int32(0)
    for j in range(lay.halo):
        row = send_row(lay, sub_ref, reg_ref, j)
        info_ref[lay.tab + j] = row
        for k in (1, 2):
            slot = slot_ref[row, k]
            info_ref[lay.out + out] = pack(j, 3 * row + k, jnp.maximum(received(slot), 0))
            out = out + jnp.where(slot < rows, 0, 1)
    for u in range(BATCH):
        info_ref[lay.out + out + u] = pack(lay.halo, 0, 0)
    info_ref[lay.n_out] = out


def gather_received(lay, got_refs, got):
    for ref, start, count in zip(got_refs, lay.starts, lay.counts):
        for j in range(count):
            got[start + j] = ref[j]


def add_received(factor, info_ref, at, count, bt_ref, got, sum_ref):
    def batch(b, carry):
        found = []
        for u in range(BATCH):
            place, block, source = unpack(info_ref[at + b * BATCH + u])
            found.append((place, dot(got[source], bt_ref[block])))
        for place, value in found:
            sum_ref[place] += factor * value
        return carry

    lax.fori_loop(0, (count + BATCH - 1) // BATCH, batch, 0)


def send_kernel(lay, factor, info_ref, bt_ref, y_ref, g0, g1, g2, g3, y_out, s0, s1, s2, s3, got, held):
    del y_out
    gather_received(lay, (g0, g1, g2, g3), got)
    for j in range(lay.halo):
        held[j] = y_ref[info_ref[lay.tab + j]]
    add_received(factor, info_ref, lay.out, info_ref[lay.n_out], bt_ref, got, held)
    for ref, start, count in zip((s0, s1, s2, s3), lay.starts, lay.counts):
        for j in range(count):
            ref[j] = held[start + j].astype(BF16)


def step_kernel(lay, step, unroll, info_ref, coeff_ref, bt_ref, g0, g1, g2, g3, x_in, y_in, t_in, ext_in,
                x_ref, y_ref, t_ref, ext_ref, got):
    del x_in, y_in, t_in, ext_in
    rows = lay.rows
    factor = 1.0 if step == 1 else 2.0
    gather_received(lay, (g0, g1, g2, g3), got)
    add_received(factor, info_ref, lay.far, info_ref[lay.n_far], bt_ref, got, y_ref)
    for i in range(rows):
        ext_ref[i] = y_ref[i].astype(BF16)
    c = coeff_ref[step]
    last = step == DEG - 1

    def many(j, carry):
        for u in range(unroll):
            i = j * unroll + u
            x = jnp.concatenate([ext_ref[info_ref[lay.loc + 3 * i + k]] for k in range(3)], 1)
            local = dot(x, bt_ref[pl.ds(3 * i, 3)].reshape(3 * 128, 128))
            base = 2.0 * local - x_ref[i]
            if last:
                t_ref[i] += c * y_ref[i] + coeff_ref[DEG] * base
            else:
                t_ref[i] += c * y_ref[i]
                x_ref[i] = base
        return carry

    lax.fori_loop(0, rows // unroll, many, 0)


def final_kernel(lay, info_ref, coeff_ref, bt_ref, t_in, g0, g1, g2, g3, out_ref, t_ref, got):
    del t_in
    gather_received(lay, (g0, g1, g2, g3), got)
    add_received(2.0 * coeff_ref[DEG], info_ref, lay.far, info_ref[lay.n_far], bt_ref, got, t_ref)
    for i in range(lay.rows):
        out_ref[:, i * 128:(i + 1) * 128] = t_ref[i]


def local(probes, blocks, col_slot, send_sub, send_reg, coeffs):
    rows, _, width, _ = blocks.shape
    count = probes.shape[0]
    lay = Layout(rows, send_sub.shape[2], send_reg.shape[2])
    chunk = divisor(rows, 13)
    unroll = divisor(rows, 52)
    small, large = 4 << 20, 20 << 20

    sends_shape = [pltpu.VMEM((n, count, width), BF16) for n in lay.counts]
    got_scratch = pltpu.VMEM((lay.halo, count, width), BF16)
    state = pltpu.VMEM((rows + 1, count, width), F32)

    sends = pl.pallas_call(
        functools.partial(first_send_kernel, lay),
        in_specs=[SMEM, SMEM, VMEM],
        out_specs=[VMEM] * 4,
        out_shape=sends_shape,
        compiler_params=pltpu.CompilerParams(vmem_limit_bytes=small),
        name="first_send",
    )(send_sub, send_reg, probes)
    got = exchange(sends)
    bt, x, y, t, ext, info = pl.pallas_call(
        functools.partial(prologue_kernel, lay, chunk),
        in_specs=[SMEM, SMEM, SMEM, SMEM, VMEM, HBM],
        out_specs=[VMEM] * 5 + [SMEM],
        out_shape=[
            pltpu.VMEM((3 * rows, width, width), BF16),
            state,
            state,
            pltpu.VMEM((rows + 1, count, width), F32),
            pltpu.VMEM((rows + 1, count, width), BF16),
            jax.ShapeDtypeStruct((lay.size,), I32),
        ],
        scratch_shapes=[pltpu.VMEM((rows, 3, width, width), BF16), pltpu.SemaphoreType.DMA((rows // chunk,))],
        compiler_params=pltpu.CompilerParams(vmem_limit_bytes=large),
        name="prologue",
    )(col_slot, send_sub, send_reg, coeffs, probes, pltpu.with_memory_space_constraint(blocks, pltpu.HBM))
    for step in range(1, DEG):
        y, *sends = pl.pallas_call(
            functools.partial(send_kernel, lay, 1.0 if step == 1 else 2.0),
            in_specs=[SMEM, VMEM, VMEM] + [VMEM] * 4,
            out_specs=[VMEM] * 5,
            out_shape=[state] + sends_shape,
            scratch_shapes=[got_scratch, pltpu.VMEM((lay.halo + 1, count, width), F32)],
            input_output_aliases={2: 0},
            compiler_params=pltpu.CompilerParams(vmem_limit_bytes=small),
            name="send",
        )(info, in_vmem(bt), in_vmem(y), *[in_vmem(g) for g in got])
        later = exchange(sends)
        x, y, t, ext = pl.pallas_call(
            functools.partial(step_kernel, lay, step, unroll),
            in_specs=[SMEM, SMEM, VMEM] + [VMEM] * 8,
            out_specs=[VMEM] * 4,
            out_shape=[state, state, state, pltpu.VMEM((rows + 1, count, width), BF16)],
            scratch_shapes=[got_scratch],
            input_output_aliases={7: 0, 8: 1, 9: 2, 10: 3},
            compiler_params=pltpu.CompilerParams(vmem_limit_bytes=small),
            cost_estimate=pl.CostEstimate(flops=2 * rows * 3 * width * width * count, bytes_accessed=1 << 20, transcendentals=0),
            name="step",
        )(info, coeffs, in_vmem(bt), *[in_vmem(g) for g in got], in_vmem(x), in_vmem(y), in_vmem(t), in_vmem(ext))
        x, y = y, x
        got = later
    out, _ = pl.pallas_call(
        functools.partial(final_kernel, lay),
        in_specs=[SMEM, SMEM, VMEM, VMEM] + [VMEM] * 4,
        out_specs=[VMEM, VMEM],
        out_shape=[jax.ShapeDtypeStruct((count, rows * width), F32), state],
        scratch_shapes=[got_scratch],
        input_output_aliases={3: 1},
        compiler_params=pltpu.CompilerParams(vmem_limit_bytes=small),
        name="final",
    )(info, coeffs, in_vmem(bt), in_vmem(t), *[in_vmem(g) for g in got])
    return out


def solution(mesh):
    return jax.shard_map(
        local,
        mesh=mesh,
        in_specs=(
            P(None, ("region", "sub")),
            P(("region", "sub"), None, None, None),
            P(("region", "sub"), None),
            P(("region", "sub"), None, None),
            P(("region", "sub"), None, None),
            P(),
        ),
        out_specs=P(None, ("region", "sub")),
        check_vma=False,
    )
```

```python
import functools

import jax
import jax.numpy as jnp
from jax import lax
from jax.experimental import pallas as pl
from jax.experimental.pallas import tpu as pltpu
from jax.sharding import PartitionSpec as P

DEG = 8
BATCH = 16
FIRST = 13
ORDER = (0, 1, 3, 2)
SMEM = pl.BlockSpec(memory_space=pltpu.SMEM)
VMEM = pl.BlockSpec(memory_space=pltpu.VMEM)
HBM = pl.BlockSpec(memory_space=pl.ANY)
F32, BF16, I32 = jnp.float32, jnp.bfloat16, jnp.int32


def dot(x, b):
    return lax.dot_general(x, b, (((1,), (0,)), ((), ())), preferred_element_type=F32)


def in_vmem(x):
    return pltpu.with_memory_space_constraint(x, pltpu.VMEM)


def in_hbm(x):
    return pltpu.with_memory_space_constraint(x, pltpu.HBM)


def in_smem(x):
    return pltpu.with_memory_space_constraint(x, pltpu.SMEM)


def divisor(n, most):
    return next(d for d in range(min(n, most), 0, -1) if n % d == 0)


def swaps():
    regions, subs = lax.axis_size("region"), lax.axis_size("sub")

    def route(mate):
        pairs = []
        for r in range(regions):
            for s in range(subs):
                m = mate(r, s)
                if m is not None:
                    pairs.append((r * subs + s, m[0] * subs + m[1]))
        return pairs

    def idle_sub(r, s):
        return (r ^ 1, s) if r ^ 1 < regions else None

    def sub_even(r, s):
        return (r, s ^ 1) if s ^ 1 < subs else idle_sub(r, s)

    def sub_odd(r, s):
        m = ((s - 1) ^ 1) + 1
        return (r, m) if s > 0 and m < subs else idle_sub(r, s)

    def reg_even(r, s):
        return (r ^ 1, s) if r ^ 1 < regions else None

    def reg_odd(r, s):
        m = ((r - 1) ^ 1) + 1
        if r > 0 and m < regions:
            return (m, s)
        return (regions - 1 - r, s) if regions % 2 == 0 else None

    return [route(f) for f in (sub_even, sub_odd, reg_even, reg_odd)]


def exchange(sends):
    routes = swaps()
    return [lax.ppermute(x, ("region", "sub"), routes[k]) for x, k in zip(sends, ORDER)]


class Layout:
    def __init__(self, rows, hs, hr):
        self.rows, self.hs, self.hr = rows, hs, hr
        self.halo = 2 * hs + 2 * hr
        self.starts = (0, hs, 2 * hs, 2 * hs + hr)
        self.counts = (hs, hs, hr, hr)
        self.loc = 0
        self.far = 3 * rows
        self.tab = self.far + 2 * rows + BATCH
        self.out = self.tab + self.halo
        self.n_far = self.out + 2 * self.halo + BATCH
        self.n_out = self.n_far + 1
        self.size = self.n_out + 1

    def lists(self, refs):
        return [(ref, self.starts[k], self.counts[k]) for ref, k in zip(refs, ORDER)]


def pack(place, block, got):
    return place + block * 1024 + got * (1 << 20)


def unpack(code):
    return code & 1023, (code >> 10) & 1023, code >> 20


def send_row(lay, sub_ref, reg_ref, j):
    rp, sp = lax.axis_index("region") % 2, lax.axis_index("sub") % 2
    hs, hr = lay.hs, lay.hr
    if j < hs:
        row = sub_ref[0, 1 - sp, j]
    elif j < 2 * hs:
        row = sub_ref[0, sp, j - hs]
    elif j < 2 * hs + hr:
        row = reg_ref[0, 1 - rp, j - 2 * hs]
    else:
        row = reg_ref[0, rp, j - 2 * hs - hr]
    return jnp.maximum(row, 0)


def first_send_kernel(lay, first, sub_hbm, reg_hbm, slot_hbm, coeff_hbm, probes_hbm, blocks_hbm,
                      s0, s1, s2, s3, sub_ref, reg_ref, slot_ref, coeff_ref, ext_ref, raw_ref, probes, sems):
    pairs = (
        (sub_hbm, sub_ref),
        (reg_hbm, reg_ref),
        (probes_hbm, probes),
        (slot_hbm, slot_ref),
        (coeff_hbm, coeff_ref),
        (blocks_hbm.at[pl.ds(0, first)], raw_ref),
    )
    loads = [pltpu.make_async_copy(a, b, sems.at[n]) for n, (a, b) in enumerate(pairs)]
    for load in loads:
        load.start()
    loads[0].wait()
    loads[1].wait()
    at = [send_row(lay, sub_ref, reg_ref, j) * 128 for j in range(lay.halo)]
    loads[2].wait()
    for ref, start, count in lay.lists((s0, s1, s2, s3)):
        for j in range(count):
            ref[j] = probes[:, pl.ds(pl.multiple_of(at[start + j], 128), 128)]
    for i in range(lay.rows):
        ext_ref[i] = probes[:, i * 128:(i + 1) * 128]
    ext_ref[lay.rows] = jnp.zeros_like(ext_ref[lay.rows])
    for load in loads[3:]:
        load.wait()


def prologue_kernel(lay, first, cuts, slot_ref, sub_ref, reg_ref, coeff_ref, ext_ref, raw0, blocks_hbm,
                    bt_ref, x_ref, y_ref, t_ref, info_ref, raw, sems):
    rows = lay.rows
    copies = [
        pltpu.make_async_copy(blocks_hbm.at[pl.ds(a, b - a)], raw.at[pl.ds(a - first, b - a)], sems.at[n])
        for n, (a, b) in enumerate(zip(cuts, cuts[1:]))
    ]
    for copy in copies:
        copy.start()
    rp, sp = lax.axis_index("region") % 2, lax.axis_index("sub") % 2
    hs, hr = lay.hs, lay.hr

    def received(slot):
        o = slot - rows
        sub_at = jnp.where(sp == 1, o, jnp.where(o < hs, o + hs, o - hs))
        q = o - 2 * hs
        reg_at = jnp.where(rp == 1, o, jnp.where(q < hr, o + hr, o - hr))
        return jnp.where(o < 2 * hs, sub_at, reg_at)

    c0 = coeff_ref[0]
    y_ref[rows] = jnp.zeros_like(y_ref[rows])
    x_ref[rows] = jnp.zeros_like(x_ref[rows])
    t_ref[rows] = jnp.zeros_like(t_ref[rows])

    def many(source, begin, end, far):
        for i in range(begin, end):
            at = []
            for k in range(3):
                slot = slot_ref[k, i]
                at.append(jnp.where(slot < rows, slot, rows))
                info_ref[lay.loc + 3 * i + k] = at[k]
                if k > 0:
                    info_ref[lay.far + far] = pack(i, 3 * i + k, jnp.maximum(received(slot), 0))
                    far = far + jnp.where(slot < rows, 0, 1)
            turned = [source(i, k).T for k in range(3)]
            for k in range(3):
                bt_ref[3 * i + k] = turned[k]
            x = jnp.concatenate([ext_ref[at[k]] for k in range(3)], 1)
            y_ref[i] = dot(x, jnp.concatenate(turned, 0))
            v = ext_ref[i].astype(F32)
            x_ref[i] = v
            t_ref[i] = c0 * v
        return far

    far = many(lambda i, k: raw0[i, k], 0, first, jnp.int32(0))
    out = jnp.int32(0)
    for j in range(lay.halo):
        row = send_row(lay, sub_ref, reg_ref, j)
        info_ref[lay.tab + j] = row
        for k in (1, 2):
            slot = slot_ref[k, row]
            info_ref[lay.out + out] = pack(j, 3 * row + k, jnp.maximum(received(slot), 0))
            out = out + jnp.where(slot < rows, 0, 1)
    for u in range(BATCH):
        info_ref[lay.out + out + u] = pack(lay.halo, 0, 0)
    info_ref[lay.n_out] = out
    for copy, a, b in zip(copies, cuts, cuts[1:]):
        copy.wait()
        far = many(lambda i, k: raw[i - first, k], a, b, far)
    for u in range(BATCH):
        info_ref[lay.far + far + u] = pack(rows, 0, 0)
    info_ref[lay.n_far] = far


def gather_received(lay, got_refs, got):
    for ref, start, count in lay.lists(got_refs):
        for j in range(count):
            got[start + j] = ref[j]


def add_received(factor, info_ref, at, count, bt_ref, got, sum_ref):
    def batch(b, carry):
        found = []
        for u in range(BATCH):
            place, block, source = unpack(info_ref[at + b * BATCH + u])
            found.append((place, dot(got[source], bt_ref[block])))
        for place, value in found:
            sum_ref[place] += factor * value
        return carry

    lax.fori_loop(0, (count + BATCH - 1) // BATCH, batch, 0)


def send_kernel(lay, factor, info_ref, bt_ref, y_ref, g0, g1, g2, g3, y_out, s0, s1, s2, s3, got, held):
    del y_out
    gather_received(lay, (g0, g1, g2, g3), got)
    for j in range(lay.halo):
        held[j] = y_ref[info_ref[lay.tab + j]]
    add_received(factor, info_ref, lay.out, info_ref[lay.n_out], bt_ref, got, held)
    for ref, start, count in lay.lists((s0, s1, s2, s3)):
        for j in range(count):
            ref[j] = held[start + j].astype(BF16)


def step_kernel(lay, step, unroll, info_ref, coeff_ref, bt_ref, g0, g1, g2, g3, x_in, y_in, t_in, ext_in,
                x_ref, y_ref, t_ref, ext_ref, got):
    del x_in, y_in, t_in, ext_in
    rows = lay.rows
    factor = 1.0 if step == 1 else 2.0
    gather_received(lay, (g0, g1, g2, g3), got)
    add_received(factor, info_ref, lay.far, info_ref[lay.n_far], bt_ref, got, y_ref)
    for i in range(rows):
        ext_ref[i] = y_ref[i].astype(BF16)
    c = coeff_ref[step]
    last = step == DEG - 1

    def many(j, carry):
        for u in range(unroll):
            i = j * unroll + u
            x = jnp.concatenate([ext_ref[info_ref[lay.loc + 3 * i + k]] for k in range(3)], 1)
            local = dot(x, bt_ref[pl.ds(3 * i, 3)].reshape(3 * 128, 128))
            base = 2.0 * local - x_ref[i]
            if last:
                t_ref[i] += c * y_ref[i] + coeff_ref[DEG] * base
            else:
                t_ref[i] += c * y_ref[i]
                x_ref[i] = base
        return carry

    lax.fori_loop(0, rows // unroll, many, 0)


def final_kernel(lay, info_ref, coeff_ref, bt_ref, t_in, g0, g1, g2, g3, out_ref, t_ref, got):
    del t_in
    gather_received(lay, (g0, g1, g2, g3), got)
    add_received(2.0 * coeff_ref[DEG], info_ref, lay.far, info_ref[lay.n_far], bt_ref, got, t_ref)
    for i in range(lay.rows):
        out_ref[:, i * 128:(i + 1) * 128] = t_ref[i]


def local(probes, blocks, col_slot, send_sub, send_reg, coeffs):
    rows, _, width, _ = blocks.shape
    count = probes.shape[0]
    lay = Layout(rows, send_sub.shape[2], send_reg.shape[2])
    unroll = divisor(rows, 52)
    small, large = 4 << 20, 20 << 20

    sends_shape = [pltpu.VMEM((n, count, width), BF16) for n in lay.counts]
    sends_shape = [sends_shape[k] for k in ORDER]
    got_scratch = pltpu.VMEM((lay.halo, count, width), BF16)
    state = pltpu.VMEM((rows + 1, count, width), F32)

    slots = col_slot.T
    first = min(FIRST, rows // 2)
    cuts = sorted(set(list(range(first, rows, 26)) + [max(first, rows - 13), rows]))
    smalls = (send_sub, send_reg, slots, coeffs)
    ext_shape = pltpu.VMEM((rows + 1, count, width), BF16)
    results = pl.pallas_call(
        functools.partial(first_send_kernel, lay, first),
        in_specs=[HBM] * 6,
        out_specs=[VMEM] * 4 + [SMEM] * 4 + [VMEM] * 2,
        out_shape=sends_shape + [pltpu.SMEM(a.shape, a.dtype) for a in smalls]
        + [ext_shape, pltpu.VMEM((first, 3, width, width), BF16)],
        scratch_shapes=[pltpu.VMEM(probes.shape, BF16), pltpu.SemaphoreType.DMA((6,))],
        compiler_params=pltpu.CompilerParams(vmem_limit_bytes=small),
        name="first_send",
    )(*[in_hbm(a) for a in smalls + (probes, blocks)])
    sends, (subs, regs, slots, coeffs, ext, raw0) = results[:4], results[4:]
    got = exchange(sends)
    bt, x, y, t, info = pl.pallas_call(
        functools.partial(prologue_kernel, lay, first, cuts),
        in_specs=[SMEM] * 4 + [VMEM] * 2 + [HBM],
        out_specs=[VMEM] * 4 + [SMEM],
        out_shape=[pltpu.VMEM((3 * rows, width, width), BF16), state, state, state, pltpu.SMEM((lay.size,), I32)],
        scratch_shapes=[pltpu.VMEM((rows - first, 3, width, width), BF16), pltpu.SemaphoreType.DMA((len(cuts) - 1,))],
        compiler_params=pltpu.CompilerParams(vmem_limit_bytes=large),
        name="prologue",
    )(*[in_smem(a) for a in (slots, subs, regs, coeffs)], in_vmem(ext), in_vmem(raw0), in_hbm(blocks))
    for step in range(1, DEG):
        y, *sends = pl.pallas_call(
            functools.partial(send_kernel, lay, 1.0 if step == 1 else 2.0),
            in_specs=[SMEM, VMEM, VMEM] + [VMEM] * 4,
            out_specs=[VMEM] * 5,
            out_shape=[state] + sends_shape,
            scratch_shapes=[got_scratch, pltpu.VMEM((lay.halo + 1, count, width), F32)],
            input_output_aliases={2: 0},
            compiler_params=pltpu.CompilerParams(vmem_limit_bytes=small),
            name="send",
        )(in_smem(info), in_vmem(bt), in_vmem(y), *[in_vmem(g) for g in got])
        later = exchange(sends)
        x, y, t, ext = pl.pallas_call(
            functools.partial(step_kernel, lay, step, unroll),
            in_specs=[SMEM, SMEM, VMEM] + [VMEM] * 8,
            out_specs=[VMEM] * 4,
            out_shape=[state, state, state, pltpu.VMEM((rows + 1, count, width), BF16)],
            scratch_shapes=[got_scratch],
            input_output_aliases={7: 0, 8: 1, 9: 2, 10: 3},
            compiler_params=pltpu.CompilerParams(vmem_limit_bytes=small),
            cost_estimate=pl.CostEstimate(flops=2 * rows * 3 * width * width * count, bytes_accessed=1 << 20, transcendentals=0),
            name="step",
        )(in_smem(info), in_smem(coeffs), in_vmem(bt), *[in_vmem(g) for g in got], in_vmem(x), in_vmem(y), in_vmem(t), in_vmem(ext))
        x, y = y, x
        got = later
    out, _ = pl.pallas_call(
        functools.partial(final_kernel, lay),
        in_specs=[SMEM, SMEM, VMEM, VMEM] + [VMEM] * 4,
        out_specs=[VMEM, VMEM],
        out_shape=[jax.ShapeDtypeStruct((count, rows * width), F32), state],
        scratch_shapes=[got_scratch],
        input_output_aliases={3: 1},
        compiler_params=pltpu.CompilerParams(vmem_limit_bytes=small),
        name="final",
    )(in_smem(info), in_smem(coeffs), in_vmem(bt), in_vmem(t), *[in_vmem(g) for g in got])
    return out


def solution(mesh):
    return jax.shard_map(
        local,
        mesh=mesh,
        in_specs=(
            P(None, ("region", "sub")),
            P(("region", "sub"), None, None, None),
            P(("region", "sub"), None),
            P(("region", "sub"), None, None),
            P(("region", "sub"), None, None),
            P(),
        ),
        out_specs=P(None, ("region", "sub")),
        check_vma=False,
    )
```

```python
import functools

import jax
import jax.numpy as jnp
from jax import lax
from jax.experimental import pallas as pl
from jax.experimental.pallas import tpu as pltpu
from jax.sharding import PartitionSpec as P

DEG = 8
BATCH = 16
ORDER = (0, 1, 3, 2)
SMEM = pl.BlockSpec(memory_space=pltpu.SMEM)
VMEM = pl.BlockSpec(memory_space=pltpu.VMEM)
HBM = pl.BlockSpec(memory_space=pl.ANY)
F32, BF16, I32 = jnp.float32, jnp.bfloat16, jnp.int32


def dot(x, b):
    return lax.dot_general(x, b, (((1,), (0,)), ((), ())), preferred_element_type=F32)


def in_vmem(x):
    return pltpu.with_memory_space_constraint(x, pltpu.VMEM)


def in_hbm(x):
    return pltpu.with_memory_space_constraint(x, pltpu.HBM)


def in_smem(x):
    return pltpu.with_memory_space_constraint(x, pltpu.SMEM)


def divisor(n, most):
    return next(d for d in range(min(n, most), 0, -1) if n % d == 0)


def swaps():
    regions, subs = lax.axis_size("region"), lax.axis_size("sub")

    def route(mate):
        pairs = []
        for r in range(regions):
            for s in range(subs):
                m = mate(r, s)
                if m is not None:
                    pairs.append((r * subs + s, m[0] * subs + m[1]))
        return pairs

    def idle_sub(r, s):
        return (r ^ 1, s) if r ^ 1 < regions else None

    def sub_even(r, s):
        return (r, s ^ 1) if s ^ 1 < subs else idle_sub(r, s)

    def sub_odd(r, s):
        m = ((s - 1) ^ 1) + 1
        return (r, m) if s > 0 and m < subs else idle_sub(r, s)

    def reg_even(r, s):
        return (r ^ 1, s) if r ^ 1 < regions else None

    def reg_odd(r, s):
        m = ((r - 1) ^ 1) + 1
        if r > 0 and m < regions:
            return (m, s)
        return (regions - 1 - r, s) if regions % 2 == 0 else None

    return [route(f) for f in (sub_even, sub_odd, reg_even, reg_odd)]


def exchange(sends):
    routes = swaps()
    return [lax.ppermute(x, ("region", "sub"), routes[k]) for x, k in zip(sends, ORDER)]


class Layout:
    def __init__(self, rows, hs, hr):
        self.rows, self.hs, self.hr = rows, hs, hr
        self.halo = 2 * hs + 2 * hr
        self.starts = (0, hs, 2 * hs, 2 * hs + hr)
        self.counts = (hs, hs, hr, hr)
        self.loc = 0
        self.far = 3 * rows
        self.n_far = self.far + 2 * rows + BATCH
        self.size = self.n_far + 1
        self.tab = 0
        self.out = self.halo
        self.n_out = self.out + 2 * self.halo + BATCH
        self.out_size = self.n_out + 1

    def lists(self, refs):
        return [(ref, self.starts[k], self.counts[k]) for ref, k in zip(refs, ORDER)]


def pack(place, block, got):
    return place + block * 1024 + got * (1 << 20)


def unpack(code):
    return code & 1023, (code >> 10) & 1023, code >> 20


def send_row(lay, sub_ref, reg_ref, j):
    rp, sp = lax.axis_index("region") % 2, lax.axis_index("sub") % 2
    hs, hr = lay.hs, lay.hr
    if j < hs:
        row = sub_ref[0, 1 - sp, j]
    elif j < 2 * hs:
        row = sub_ref[0, sp, j - hs]
    elif j < 2 * hs + hr:
        row = reg_ref[0, 1 - rp, j - 2 * hs]
    else:
        row = reg_ref[0, rp, j - 2 * hs - hr]
    return jnp.maximum(row, 0)


def received_place(lay, slot):
    rp, sp = lax.axis_index("region") % 2, lax.axis_index("sub") % 2
    hs, hr = lay.hs, lay.hr
    o = slot - lay.rows
    sub_at = jnp.where(sp == 1, o, jnp.where(o < hs, o + hs, o - hs))
    q = o - 2 * hs
    reg_at = jnp.where(rp == 1, o, jnp.where(q < hr, o + hr, o - hr))
    return jnp.maximum(jnp.where(o < 2 * hs, sub_at, reg_at), 0)


def first_send_kernel(lay, first, sub_hbm, reg_hbm, slot_hbm, coeff_hbm, probes_hbm, blocks_hbm,
                      s0, s1, s2, s3, slot_ref, coeff_ref, out_info, ext_ref, raw_ref, probes, sub_ref, reg_ref, sems):
    pairs = (
        (sub_hbm, sub_ref),
        (reg_hbm, reg_ref),
        (slot_hbm, slot_ref),
        (probes_hbm, probes),
        (coeff_hbm, coeff_ref),
        (blocks_hbm.at[pl.ds(0, first)], raw_ref.at[pl.ds(0, first)]),
    )
    loads = [pltpu.make_async_copy(a, b, sems.at[n]) for n, (a, b) in enumerate(pairs)]
    for load in loads:
        load.start()
    for load in loads[:3]:
        load.wait()
    at = []
    out = jnp.int32(0)
    for j in range(lay.halo):
        row = send_row(lay, sub_ref, reg_ref, j)
        at.append(row * 128)
        out_info[lay.tab + j] = row
        for k in (1, 2):
            slot = slot_ref[k, row]
            out_info[lay.out + out] = pack(j, 3 * row + k, received_place(lay, slot))
            out = out + jnp.where(slot < lay.rows, 0, 1)
    for u in range(BATCH):
        out_info[lay.out + out + u] = pack(lay.halo, 0, 0)
    out_info[lay.n_out] = out
    loads[3].wait()
    for ref, start, count in lay.lists((s0, s1, s2, s3)):
        for j in range(count):
            ref[j] = probes[:, pl.ds(pl.multiple_of(at[start + j], 128), 128)]
    for i in range(lay.rows):
        ext_ref[i] = probes[:, i * 128:(i + 1) * 128]
    ext_ref[lay.rows] = jnp.zeros_like(ext_ref[lay.rows])
    for load in loads[4:]:
        load.wait()


def prologue_kernel(lay, chunk, slot_ref, ext_ref, raw_in, blocks_hbm, bt_ref, y_ref, raw, info_ref, sems):
    del raw_in
    rows = lay.rows
    chunks = rows // chunk

    def load(c):
        part = pl.ds(c * chunk, chunk)
        return pltpu.make_async_copy(blocks_hbm.at[part], raw.at[part], sems.at[c])

    for c in range(1, chunks):
        load(c).start()
    y_ref[rows] = jnp.zeros_like(y_ref[rows])

    def many(c, far):
        @pl.when(c > 0)
        def _():
            load(c).wait()

        for u in range(chunk):
            i = c * chunk + u
            at = []
            for k in range(3):
                slot = slot_ref[k, i]
                at.append(jnp.where(slot < rows, slot, rows))
                info_ref[lay.loc + 3 * i + k] = at[k]
                if k > 0:
                    info_ref[lay.far + far] = pack(i, 3 * i + k, received_place(lay, slot))
                    far = far + jnp.where(slot < rows, 0, 1)
            turned = [raw[i, k].T for k in range(3)]
            for k in range(3):
                bt_ref[3 * i + k] = turned[k]
            x = jnp.concatenate([ext_ref[at[k]] for k in range(3)], 1)
            y_ref[i] = dot(x, jnp.concatenate(turned, 0))
        return far

    far = lax.fori_loop(0, chunks, many, jnp.int32(0))
    for u in range(BATCH):
        info_ref[lay.far + far + u] = pack(rows, 0, 0)
    info_ref[lay.n_far] = far


def gather_received(lay, got_refs, got):
    for ref, start, count in lay.lists(got_refs):
        for j in range(count):
            got[start + j] = ref[j]


def add_received(factor, info_ref, at, count, bt_ref, got, sum_ref):
    def batch(b, carry):
        found = []
        for u in range(BATCH):
            place, block, source = unpack(info_ref[at + b * BATCH + u])
            found.append((place, dot(got[source], bt_ref[block])))
        for place, value in found:
            sum_ref[place] += factor * value
        return carry

    lax.fori_loop(0, (count + BATCH - 1) // BATCH, batch, 0)


def send_kernel(lay, factor, info_ref, bt_ref, y_ref, g0, g1, g2, g3, y_out, s0, s1, s2, s3, got, held):
    del y_out
    gather_received(lay, (g0, g1, g2, g3), got)
    for j in range(lay.halo):
        held[j] = y_ref[info_ref[lay.tab + j]]
    add_received(factor, info_ref, lay.out, info_ref[lay.n_out], bt_ref, got, held)
    for ref, start, count in lay.lists((s0, s1, s2, s3)):
        for j in range(count):
            ref[j] = held[start + j].astype(BF16)


def step_kernel(lay, step, unroll, info_ref, coeff_ref, bt_ref, g0, g1, g2, g3, *refs):
    rows = lay.rows
    first, last = step == 1, step == DEG - 1
    if first:
        y_in, p_ref, x_ref, y_ref, t_ref, ext_ref, got = refs
    else:
        x_in, y_in, t_in, ext_in, x_ref, y_ref, t_ref, ext_ref, got = refs
    del y_in
    factor = 1.0 if first else 2.0
    gather_received(lay, (g0, g1, g2, g3), got)
    add_received(factor, info_ref, lay.far, info_ref[lay.n_far], bt_ref, got, y_ref)
    for i in range(rows):
        ext_ref[i] = y_ref[i].astype(BF16)
    if first:
        ext_ref[rows] = jnp.zeros_like(ext_ref[rows])
        t_ref[rows] = jnp.zeros_like(t_ref[rows])
        x_ref[rows] = jnp.zeros_like(x_ref[rows])
    c = coeff_ref[step]

    def many(j, carry):
        for u in range(unroll):
            i = j * unroll + u
            x = jnp.concatenate([ext_ref[info_ref[lay.loc + 3 * i + k]] for k in range(3)], 1)
            local = dot(x, bt_ref[pl.ds(3 * i, 3)].reshape(3 * 128, 128))
            if first:
                old = p_ref[i].astype(F32)
                t_ref[i] = coeff_ref[0] * old + c * y_ref[i]
                x_ref[i] = 2.0 * local - old
            elif last:
                t_ref[i] += c * y_ref[i] + coeff_ref[DEG] * (2.0 * local - x_ref[i])
            else:
                t_ref[i] += c * y_ref[i]
                x_ref[i] = 2.0 * local - x_ref[i]
        return carry

    lax.fori_loop(0, rows // unroll, many, 0)


def final_kernel(lay, part, info_ref, coeff_ref, bt_ref, t_in, g0, g1, g2, g3, out_hbm, t_ref, got, wide, sems):
    del t_in
    gather_received(lay, (g0, g1, g2, g3), got)
    add_received(2.0 * coeff_ref[DEG], info_ref, lay.far, info_ref[lay.n_far], bt_ref, got, t_ref)
    copies = []
    for j in range(lay.rows // part):
        for i in range(j * part, (j + 1) * part):
            wide[:, i * 128:(i + 1) * 128] = t_ref[i]
        columns = pl.ds(j * part * 128, part * 128)
        copies.append(pltpu.make_async_copy(wide.at[:, columns], out_hbm.at[:, columns], sems.at[j]))
        copies[-1].start()
    for copy in copies:
        copy.wait()


def local(probes, blocks, col_slot, send_sub, send_reg, coeffs):
    rows, _, width, _ = blocks.shape
    count = probes.shape[0]
    lay = Layout(rows, send_sub.shape[2], send_reg.shape[2])
    unroll = divisor(rows, 52)
    small = 4 << 20

    sends_shape = [pltpu.VMEM((n, count, width), BF16) for n in lay.counts]
    sends_shape = [sends_shape[k] for k in ORDER]
    got_scratch = pltpu.VMEM((lay.halo, count, width), BF16)
    state = pltpu.VMEM((rows + 1, count, width), F32)

    slots = col_slot.T
    chunk = divisor(rows, 26)
    part = divisor(rows, 26)
    ext_shape = pltpu.VMEM((rows + 1, count, width), BF16)
    results = pl.pallas_call(
        functools.partial(first_send_kernel, lay, chunk),
        in_specs=[HBM] * 6,
        out_specs=[VMEM] * 4 + [SMEM] * 3 + [VMEM] * 2,
        out_shape=sends_shape + [
            pltpu.SMEM(slots.shape, I32),
            pltpu.SMEM(coeffs.shape, F32),
            pltpu.SMEM((lay.out_size,), I32),
            ext_shape,
            pltpu.VMEM(blocks.shape, BF16),
        ],
        scratch_shapes=[
            pltpu.VMEM(probes.shape, BF16),
            pltpu.SMEM(send_sub.shape, I32),
            pltpu.SMEM(send_reg.shape, I32),
            pltpu.SemaphoreType.DMA((6,)),
        ],
        compiler_params=pltpu.CompilerParams(vmem_limit_bytes=small),
        name="first_send",
    )(*[in_hbm(a) for a in (send_sub, send_reg, slots, coeffs, probes, blocks)])
    sends, (slots, coeffs, out_info, start, raw0) = results[:4], results[4:]
    coeffs = in_smem(coeffs)
    got = exchange(sends)
    bt, y, _, info = pl.pallas_call(
        functools.partial(prologue_kernel, lay, chunk),
        in_specs=[SMEM] + [VMEM] * 2 + [HBM],
        out_specs=[VMEM] * 3 + [SMEM],
        out_shape=[
            pltpu.VMEM((3 * rows, width, width), BF16),
            state,
            pltpu.VMEM(blocks.shape, BF16),
            pltpu.SMEM((lay.size,), I32),
        ],
        scratch_shapes=[pltpu.SemaphoreType.DMA((rows // chunk,))],
        input_output_aliases={2: 2},
        compiler_params=pltpu.CompilerParams(vmem_limit_bytes=small),
        name="prologue",
    )(in_smem(slots), in_vmem(start), in_vmem(raw0), in_hbm(blocks))
    info, bt = in_smem(info), in_vmem(bt)
    for step in range(1, DEG):
        y, *sends = pl.pallas_call(
            functools.partial(send_kernel, lay, 1.0 if step == 1 else 2.0),
            in_specs=[SMEM, VMEM, VMEM] + [VMEM] * 4,
            out_specs=[VMEM] * 5,
            out_shape=[state] + sends_shape,
            scratch_shapes=[got_scratch, pltpu.VMEM((lay.halo + 1, count, width), F32)],
            input_output_aliases={2: 0},
            compiler_params=pltpu.CompilerParams(vmem_limit_bytes=small),
            name="send",
        )(in_smem(out_info), bt, in_vmem(y), *[in_vmem(g) for g in got])
        later = exchange(sends)
        if step == 1:
            states, aliases = [y, start], {7: 1}
        else:
            states, aliases = [x, y, t, ext], {7: 0, 8: 1, 9: 2, 10: 3}
        x, y, t, ext = pl.pallas_call(
            functools.partial(step_kernel, lay, step, unroll),
            in_specs=[SMEM, SMEM, VMEM] + [VMEM] * (4 + len(states)),
            out_specs=[VMEM] * 4,
            out_shape=[state, state, state, ext_shape],
            scratch_shapes=[got_scratch],
            input_output_aliases=aliases,
            compiler_params=pltpu.CompilerParams(vmem_limit_bytes=small),
            cost_estimate=pl.CostEstimate(flops=2 * rows * 3 * width * width * count, bytes_accessed=1 << 20, transcendentals=0),
            name="step",
        )(info, coeffs, bt, *[in_vmem(g) for g in got], *[in_vmem(a) for a in states])
        x, y = y, x
        got = later
    out, _ = pl.pallas_call(
        functools.partial(final_kernel, lay, part),
        in_specs=[SMEM, SMEM, VMEM, VMEM] + [VMEM] * 4,
        out_specs=[HBM, VMEM],
        out_shape=[jax.ShapeDtypeStruct((count, rows * width), F32), state],
        scratch_shapes=[got_scratch, pltpu.VMEM((count, rows * width), F32), pltpu.SemaphoreType.DMA((rows // part,))],
        input_output_aliases={3: 1},
        compiler_params=pltpu.CompilerParams(vmem_limit_bytes=small),
        name="final",
    )(info, coeffs, bt, in_vmem(t), *[in_vmem(g) for g in got])
    return out


def solution(mesh):
    return jax.shard_map(
        local,
        mesh=mesh,
        in_specs=(
            P(None, ("region", "sub")),
            P(("region", "sub"), None, None, None),
            P(("region", "sub"), None),
            P(("region", "sub"), None, None),
            P(("region", "sub"), None, None),
            P(),
        ),
        out_specs=P(None, ("region", "sub")),
        check_vma=False,
    )
```

```python
import functools

import jax
import jax.numpy as jnp
from jax import lax
from jax.experimental import pallas as pl
from jax.experimental.pallas import tpu as pltpu
from jax.sharding import PartitionSpec as P

DEG = 8
BATCH = 16
ORDER = (0, 1, 3, 2)
SMEM = pl.BlockSpec(memory_space=pltpu.SMEM)
VMEM = pl.BlockSpec(memory_space=pltpu.VMEM)
HBM = pl.BlockSpec(memory_space=pl.ANY)
F32, BF16, I32 = jnp.float32, jnp.bfloat16, jnp.int32


def dot(x, b):
    return lax.dot_general(x, b, (((1,), (0,)), ((), ())), preferred_element_type=F32)


def in_vmem(x):
    return pltpu.with_memory_space_constraint(x, pltpu.VMEM)


def in_hbm(x):
    return pltpu.with_memory_space_constraint(x, pltpu.HBM)


def in_smem(x):
    return pltpu.with_memory_space_constraint(x, pltpu.SMEM)


def divisor(n, most):
    return next(d for d in range(min(n, most), 0, -1) if n % d == 0)


def swaps():
    regions, subs = lax.axis_size("region"), lax.axis_size("sub")

    def route(mate):
        pairs = []
        for r in range(regions):
            for s in range(subs):
                m = mate(r, s)
                if m is not None:
                    pairs.append((r * subs + s, m[0] * subs + m[1]))
        return pairs

    def idle_sub(r, s):
        return (r ^ 1, s) if r ^ 1 < regions else None

    def sub_even(r, s):
        return (r, s ^ 1) if s ^ 1 < subs else idle_sub(r, s)

    def sub_odd(r, s):
        m = ((s - 1) ^ 1) + 1
        return (r, m) if s > 0 and m < subs else idle_sub(r, s)

    def reg_even(r, s):
        return (r ^ 1, s) if r ^ 1 < regions else None

    def reg_odd(r, s):
        m = ((r - 1) ^ 1) + 1
        if r > 0 and m < regions:
            return (m, s)
        return (regions - 1 - r, s) if regions % 2 == 0 else None

    return [route(f) for f in (sub_even, sub_odd, reg_even, reg_odd)]


def exchange(sends):
    routes = swaps()
    return [lax.ppermute(x, ("region", "sub"), routes[k]) for x, k in zip(sends, ORDER)]


class Layout:
    def __init__(self, rows, hs, hr):
        self.rows, self.hs, self.hr = rows, hs, hr
        self.halo = 2 * hs + 2 * hr
        self.starts = (0, hs, 2 * hs, 2 * hs + hr)
        self.counts = (hs, hs, hr, hr)
        self.loc = 0
        self.far = 3 * rows
        self.n_far = self.far + 2 * rows + BATCH
        self.size = self.n_far + 1
        self.tab = 0
        self.out = self.halo
        self.n_out = self.out + 2 * self.halo + BATCH
        self.out_size = self.n_out + 1

    def lists(self, refs):
        return [(ref, self.starts[k], self.counts[k]) for ref, k in zip(refs, ORDER)]


def pack(place, block, got):
    return place + block * 1024 + got * (1 << 20)


def unpack(code):
    return code & 1023, (code >> 10) & 1023, code >> 20


def send_row(lay, sub_ref, reg_ref, j):
    rp, sp = lax.axis_index("region") % 2, lax.axis_index("sub") % 2
    hs, hr = lay.hs, lay.hr
    if j < hs:
        row = sub_ref[0, 1 - sp, j]
    elif j < 2 * hs:
        row = sub_ref[0, sp, j - hs]
    elif j < 2 * hs + hr:
        row = reg_ref[0, 1 - rp, j - 2 * hs]
    else:
        row = reg_ref[0, rp, j - 2 * hs - hr]
    return jnp.maximum(row, 0)


def received_place(lay, slot):
    rp, sp = lax.axis_index("region") % 2, lax.axis_index("sub") % 2
    hs, hr = lay.hs, lay.hr
    o = slot - lay.rows
    sub_at = jnp.where(sp == 1, o, jnp.where(o < hs, o + hs, o - hs))
    q = o - 2 * hs
    reg_at = jnp.where(rp == 1, o, jnp.where(q < hr, o + hr, o - hr))
    return jnp.maximum(jnp.where(o < 2 * hs, sub_at, reg_at), 0)


def first_send_kernel(lay, sub_hbm, reg_hbm, slot_hbm, coeff_hbm, probes_hbm,
                      s0, s1, s2, s3, slot_ref, coeff_ref, out_info, ext_ref, probes, sub_ref, reg_ref, sems):
    pairs = (
        (sub_hbm, sub_ref),
        (reg_hbm, reg_ref),
        (slot_hbm, slot_ref),
        (probes_hbm, probes),
        (coeff_hbm, coeff_ref),
    )
    loads = [pltpu.make_async_copy(a, b, sems.at[n]) for n, (a, b) in enumerate(pairs)]
    for load in loads:
        load.start()
    for load in loads[:3]:
        load.wait()
    at = []
    out = jnp.int32(0)
    for j in range(lay.halo):
        row = send_row(lay, sub_ref, reg_ref, j)
        at.append(row * 128)
        out_info[lay.tab + j] = row
        for k in (1, 2):
            slot = slot_ref[k, row]
            out_info[lay.out + out] = pack(j, 3 * row + k, received_place(lay, slot))
            out = out + jnp.where(slot < lay.rows, 0, 1)
    for u in range(BATCH):
        out_info[lay.out + out + u] = pack(lay.halo, 0, 0)
    out_info[lay.n_out] = out
    loads[3].wait()
    for ref, start, count in lay.lists((s0, s1, s2, s3)):
        for j in range(count):
            ref[j] = probes[:, pl.ds(pl.multiple_of(at[start + j], 128), 128)]
    for i in range(lay.rows):
        ext_ref[i] = probes[:, i * 128:(i + 1) * 128]
    ext_ref[lay.rows] = jnp.zeros_like(ext_ref[lay.rows])
    for load in loads[4:]:
        load.wait()


def prologue_kernel(lay, chunk, slot_ref, ext_ref, raw, bt_ref, y_ref, info_ref):
    rows = lay.rows
    chunks = rows // chunk
    y_ref[rows] = jnp.zeros_like(y_ref[rows])

    def many(c, far):
        for u in range(chunk):
            i = c * chunk + u
            at = []
            for k in range(3):
                slot = slot_ref[k, i]
                at.append(jnp.where(slot < rows, slot, rows))
                info_ref[lay.loc + 3 * i + k] = at[k]
                if k > 0:
                    info_ref[lay.far + far] = pack(i, 3 * i + k, received_place(lay, slot))
                    far = far + jnp.where(slot < rows, 0, 1)
            turned = [raw[i, k].T for k in range(3)]
            for k in range(3):
                bt_ref[3 * i + k] = turned[k]
            x = jnp.concatenate([ext_ref[at[k]] for k in range(3)], 1)
            y_ref[i] = dot(x, jnp.concatenate(turned, 0))
        return far

    far = lax.fori_loop(0, chunks, many, jnp.int32(0))
    for u in range(BATCH):
        info_ref[lay.far + far + u] = pack(rows, 0, 0)
    info_ref[lay.n_far] = far


def gather_received(lay, got_refs, got):
    for ref, start, count in lay.lists(got_refs):
        for j in range(count):
            got[start + j] = ref[j]


def add_received(factor, info_ref, at, count, bt_ref, got, sum_ref):
    def batch(b, carry):
        found = []
        for u in range(BATCH):
            place, block, source = unpack(info_ref[at + b * BATCH + u])
            found.append((place, dot(got[source], bt_ref[block])))
        for place, value in found:
            sum_ref[place] += factor * value
        return carry

    lax.fori_loop(0, (count + BATCH - 1) // BATCH, batch, 0)


def send_kernel(lay, factor, info_ref, bt_ref, y_ref, g0, g1, g2, g3, y_out, s0, s1, s2, s3, got, held):
    del y_out
    gather_received(lay, (g0, g1, g2, g3), got)
    for j in range(lay.halo):
        held[j] = y_ref[info_ref[lay.tab + j]]
    add_received(factor, info_ref, lay.out, info_ref[lay.n_out], bt_ref, got, held)
    for ref, start, count in lay.lists((s0, s1, s2, s3)):
        for j in range(count):
            ref[j] = held[start + j].astype(BF16)


def step_kernel(lay, step, unroll, info_ref, coeff_ref, bt_ref, g0, g1, g2, g3, *refs):
    rows = lay.rows
    first, last = step == 1, step == DEG - 1
    if first:
        y_in, p_ref, x_ref, y_ref, t_ref, ext_ref, got = refs
    else:
        x_in, y_in, t_in, ext_in, x_ref, y_ref, t_ref, ext_ref, got = refs
    del y_in
    factor = 1.0 if first else 2.0
    gather_received(lay, (g0, g1, g2, g3), got)
    add_received(factor, info_ref, lay.far, info_ref[lay.n_far], bt_ref, got, y_ref)
    for i in range(rows):
        ext_ref[i] = y_ref[i].astype(BF16)
    if first:
        ext_ref[rows] = jnp.zeros_like(ext_ref[rows])
        t_ref[rows] = jnp.zeros_like(t_ref[rows])
        x_ref[rows] = jnp.zeros_like(x_ref[rows])
    c = coeff_ref[step]

    def many(j, carry):
        for u in range(unroll):
            i = j * unroll + u
            x = jnp.concatenate([ext_ref[info_ref[lay.loc + 3 * i + k]] for k in range(3)], 1)
            local = dot(x, bt_ref[pl.ds(3 * i, 3)].reshape(3 * 128, 128))
            if first:
                old = p_ref[i].astype(F32)
                t_ref[i] = coeff_ref[0] * old + c * y_ref[i]
                x_ref[i] = 2.0 * local - old
            elif last:
                t_ref[i] += c * y_ref[i] + coeff_ref[DEG] * (2.0 * local - x_ref[i])
            else:
                t_ref[i] += c * y_ref[i]
                x_ref[i] = 2.0 * local - x_ref[i]
        return carry

    lax.fori_loop(0, rows // unroll, many, 0)


def final_kernel(lay, part, info_ref, coeff_ref, bt_ref, t_in, g0, g1, g2, g3, out_hbm, t_ref, got, wide, sems):
    del t_in
    gather_received(lay, (g0, g1, g2, g3), got)
    add_received(2.0 * coeff_ref[DEG], info_ref, lay.far, info_ref[lay.n_far], bt_ref, got, t_ref)
    copies = []
    for j in range(lay.rows // part):
        for i in range(j * part, (j + 1) * part):
            wide[:, i * 128:(i + 1) * 128] = t_ref[i]
        columns = pl.ds(j * part * 128, part * 128)
        copies.append(pltpu.make_async_copy(wide.at[:, columns], out_hbm.at[:, columns], sems.at[j]))
        copies[-1].start()
    for copy in copies:
        copy.wait()


def local(probes, blocks, col_slot, send_sub, send_reg, coeffs):
    rows, _, width, _ = blocks.shape
    count = probes.shape[0]
    lay = Layout(rows, send_sub.shape[2], send_reg.shape[2])
    unroll = divisor(rows, 52)
    small = 4 << 20

    sends_shape = [pltpu.VMEM((n, count, width), BF16) for n in lay.counts]
    sends_shape = [sends_shape[k] for k in ORDER]
    got_scratch = pltpu.VMEM((lay.halo, count, width), BF16)
    state = pltpu.VMEM((rows + 1, count, width), F32)

    slots = col_slot.T
    chunk = divisor(rows, 26)
    part = divisor(rows, 26)
    ext_shape = pltpu.VMEM((rows + 1, count, width), BF16)
    results = pl.pallas_call(
        functools.partial(first_send_kernel, lay),
        in_specs=[HBM] * 5,
        out_specs=[VMEM] * 4 + [SMEM] * 3 + [VMEM],
        out_shape=sends_shape + [
            pltpu.SMEM(slots.shape, I32),
            pltpu.SMEM(coeffs.shape, F32),
            pltpu.SMEM((lay.out_size,), I32),
            ext_shape,
        ],
        scratch_shapes=[
            pltpu.VMEM(probes.shape, BF16),
            pltpu.SMEM(send_sub.shape, I32),
            pltpu.SMEM(send_reg.shape, I32),
            pltpu.SemaphoreType.DMA((5,)),
        ],
        compiler_params=pltpu.CompilerParams(vmem_limit_bytes=small),
        cost_estimate=pl.CostEstimate(flops=10**10, bytes_accessed=60 << 20, transcendentals=0),
        name="first_send",
    )(*[in_hbm(a) for a in (send_sub, send_reg, slots, coeffs, probes)])
    sends, (slots, coeffs, out_info, start) = results[:4], results[4:]
    coeffs = in_smem(coeffs)
    got = exchange(sends)
    bt, y, info = pl.pallas_call(
        functools.partial(prologue_kernel, lay, chunk),
        in_specs=[SMEM] + [VMEM] * 2,
        out_specs=[VMEM] * 2 + [SMEM],
        out_shape=[pltpu.VMEM((3 * rows, width, width), BF16), state, pltpu.SMEM((lay.size,), I32)],
        compiler_params=pltpu.CompilerParams(vmem_limit_bytes=28 << 20),
        name="prologue",
    )(in_smem(slots), in_vmem(start), blocks)
    info, bt = in_smem(info), in_vmem(bt)
    for step in range(1, DEG):
        y, *sends = pl.pallas_call(
            functools.partial(send_kernel, lay, 1.0 if step == 1 else 2.0),
            in_specs=[SMEM, VMEM, VMEM] + [VMEM] * 4,
            out_specs=[VMEM] * 5,
            out_shape=[state] + sends_shape,
            scratch_shapes=[got_scratch, pltpu.VMEM((lay.halo + 1, count, width), F32)],
            input_output_aliases={2: 0},
            compiler_params=pltpu.CompilerParams(vmem_limit_bytes=small),
            name="send",
        )(in_smem(out_info), bt, in_vmem(y), *[in_vmem(g) for g in got])
        later = exchange(sends)
        if step == 1:
            states, aliases = [y, start], {7: 1}
        else:
            states, aliases = [x, y, t, ext], {7: 0, 8: 1, 9: 2, 10: 3}
        x, y, t, ext = pl.pallas_call(
            functools.partial(step_kernel, lay, step, unroll),
            in_specs=[SMEM, SMEM, VMEM] + [VMEM] * (4 + len(states)),
            out_specs=[VMEM] * 4,
            out_shape=[state, state, state, ext_shape],
            scratch_shapes=[got_scratch],
            input_output_aliases=aliases,
            compiler_params=pltpu.CompilerParams(vmem_limit_bytes=small),
            cost_estimate=pl.CostEstimate(flops=2 * rows * 3 * width * width * count, bytes_accessed=1 << 20, transcendentals=0),
            name="step",
        )(info, coeffs, bt, *[in_vmem(g) for g in got], *[in_vmem(a) for a in states])
        x, y = y, x
        got = later
    out, _ = pl.pallas_call(
        functools.partial(final_kernel, lay, part),
        in_specs=[SMEM, SMEM, VMEM, VMEM] + [VMEM] * 4,
        out_specs=[HBM, VMEM],
        out_shape=[jax.ShapeDtypeStruct((count, rows * width), F32), state],
        scratch_shapes=[got_scratch, pltpu.VMEM((count, rows * width), F32), pltpu.SemaphoreType.DMA((rows // part,))],
        input_output_aliases={3: 1},
        compiler_params=pltpu.CompilerParams(vmem_limit_bytes=small),
        name="final",
    )(info, coeffs, bt, in_vmem(t), *[in_vmem(g) for g in got])
    return out


def solution(mesh):
    return jax.shard_map(
        local,
        mesh=mesh,
        in_specs=(
            P(None, ("region", "sub")),
            P(("region", "sub"), None, None, None),
            P(("region", "sub"), None),
            P(("region", "sub"), None, None),
            P(("region", "sub"), None, None),
            P(),
        ),
        out_specs=P(None, ("region", "sub")),
        check_vma=False,
    )
```
